32 devices in a mesh: tm: 8 (over z, x), rows: 4 (over y, core).
Axes of the slice: x: 2, y: 2, z: 4, core: 2. Of those that a mesh axis runs over, the one named last changes fastest.
Arguments:
- tile_values: bfloat16 [16384, 128, 128], P(('tm', 'rows')), may hold values from -6 to 6
- tile_users: int32 [16384], P(('tm', 'rows')), may hold values from 0 to 31
- tile_items: int32 [16384], P(('tm', 'rows')), may hold values from 0 to 31
- tile_steps: int32 [16384], P(('tm', 'rows')), may hold values from 0 to 7
- tile_count: int32 [32], P(('tm', 'rows')), may hold values from 64 to 512, as said below
- users_ask: int32 [1024, 1], P(('tm', 'rows')), may hold values from 0 to 7, as said below
- items_ask: int32 [1024, 1], P(('tm', 'rows')), may hold values from 0 to 7, as said below
- user_factor: float32 [256, 64, 128], P(('tm', 'rows')), may hold values from -6 to 6
- item_factor: float32 [256, 64, 128], P(('tm', 'rows')), may hold values from -6 to 6
- time_factor: float32 [64, 64], P('tm'), may hold values from -2 to 2
- core: float32 [64, 64, 64], replicated, may hold values from -0.25 to 0.25
Outputs:
- grad_users: float32 [256, 64, 128], P(('tm', 'rows'))
- grad_items: float32 [256, 64, 128], P(('tm', 'rows'))
- grad_time: float32 [64, 64], P('tm')
- grad_core: float32 [64, 64, 64], replicated
The draws below stay inside these ranges and needn't reach their ends.
Inputs may be any that keep to these rules, and one draw needn't show every extreme that they name: `users_ask`: each row holds 1 distinct local block numbers of the owner that the row names. `items_ask`: each row holds 1 distinct local block numbers of the owner that the row names. `tile_count`: slots of a device at or past its count are padding; some device is full.
All inputs are finite; a program needn't handle non-finite values.
Results may differ from the reference program's by a relative error of at most 0.0003.
Values sent between devices are 32-bit elements; how exact they have to be, the bound alone decides.
A program may use at most 128 MiB of HBM per device.

```python
import jax
import jax.numpy as jnp
from jax import lax

RANK = 64
BLOCK = 128
TILE_DEV = 512
BLOCKS_DEV = 8
STEP_DEV = 8
CAP = 1
OWNERS = 32
NB = 256
TILES = 16384
STEPS = 64
N_ROWS = 4


def pick_rows(key):
    row_keys = jax.random.split(key, OWNERS * OWNERS)

    def pick_one(row_key):
        return jax.random.permutation(row_key, BLOCKS_DEV)[:CAP]
    return jax.vmap(pick_one)(row_keys).astype(jnp.int32)


def draw_users_ask(key, part):
    key = jax.random.fold_in(key, 1)
    return pick_rows(key)


def draw_items_ask(key, part):
    key = jax.random.fold_in(key, 2)
    return pick_rows(key)


def draw_tile_count(key, part):
    key = jax.random.fold_in(key, 3)
    powers = jax.random.randint(key, (OWNERS,), 0, 4)
    counts = TILE_DEV // jnp.left_shift(jnp.ones((OWNERS,), jnp.int32), powers.astype(jnp.int32))
    fullest = jax.random.randint(jax.random.fold_in(key, 7), (), 0, OWNERS)
    return counts.at[fullest].set(TILE_DEV).astype(jnp.int32)


def with_ends(drawn, own_key, smallest, largest):
    place = [jax.random.randint(jax.random.fold_in(own_key, axis), (), 0, length) for axis, length in enumerate(drawn.shape)]
    longest = drawn.shape.index(max(drawn.shape))
    next_to = place[:longest] + [(place[longest] + 1) % drawn.shape[longest]] + place[longest + 1:]
    return drawn.at[tuple(place)].set(smallest).at[tuple(next_to)].set(largest)


def shard_levels(rng, extent, cuts, least, largest):
    level, own = 1.0, jax.random.fold_in(rng, 6)
    for axis_at, shards_of in cuts:
        heights = jnp.exp(jax.random.uniform(jax.random.fold_in(own, axis_at), (shards_of,), jnp.float32, least / len(cuts), largest / len(cuts)))
        level = level * jnp.repeat(heights, extent[axis_at] // shards_of).reshape([-1 if axis == axis_at else 1 for axis in range(len(extent))])
    return level


def gaussian(own_key, dims, deviation, most, shards=(), kind=jnp.bfloat16):
    entries = deviation * jax.random.normal(own_key, dims, jnp.float32)
    if shards:
        entries = entries * shard_levels(own_key, dims, shards, -0.22, 0.18)
    return jnp.clip(entries, -most, most).astype(kind)


def setup_inputs(seed: int = 0) -> dict:
    key_of = jax.random.split(jax.random.key(seed), 12)
    return {
        "tile_values": gaussian(key_of[0], (TILES, BLOCK, BLOCK), 1.0, 6.0, ((0, 32),)),
        "tile_users": with_ends(jax.random.randint(key_of[1], (TILES,), 0, OWNERS * CAP), jax.random.fold_in(key_of[1], 1), 0, (OWNERS * CAP) - 1).astype(jnp.int32),
        "tile_items": with_ends(jax.random.randint(key_of[2], (TILES,), 0, OWNERS * CAP), jax.random.fold_in(key_of[2], 1), 0, (OWNERS * CAP) - 1).astype(jnp.int32),
        "tile_steps": with_ends(jax.random.randint(key_of[3], (TILES,), 0, STEP_DEV), jax.random.fold_in(key_of[3], 1), 0, STEP_DEV - 1).astype(jnp.int32),
        "tile_count": draw_tile_count(jax.random.fold_in(key_of[11], 71), 0),
        "users_ask": draw_users_ask(jax.random.fold_in(key_of[11], 71), 0),
        "items_ask": draw_items_ask(jax.random.fold_in(key_of[11], 71), 0),
        "user_factor": gaussian(key_of[7], (NB, RANK, BLOCK), 1.0, 6.0, ((0, 32),), jnp.float32),
        "item_factor": gaussian(key_of[8], (NB, RANK, BLOCK), 1.0, 6.0, ((0, 32),), jnp.float32),
        "time_factor": gaussian(key_of[9], (STEPS, RANK), (RANK ** -0.5), 2.0, ((0, 8),), jnp.float32),
        "core": gaussian(key_of[10], (RANK, RANK, RANK), (1.0 / RANK), 0.25, (), jnp.float32),
    }


HIGH = lax.Precision.HIGHEST
user_scale = 0.125
time_scale = 1.0 / 2048.0
core_scale = 1.0 / 4096.0


def reference(tile_values, tile_users, tile_items, tile_steps, tile_count, users_ask, items_ask, user_factor, item_factor, time_factor, core):
    asks_user = users_ask.reshape(OWNERS, OWNERS * CAP)
    asks_item = items_ask.reshape(OWNERS, OWNERS * CAP)

    def visit(carry, device):
        grad_left, grad_right, step_sums = carry
        start = device * TILE_DEV
        values = lax.dynamic_slice_in_dim(tile_values, start, TILE_DEV, 0).astype(jnp.float32)
        slots_user = lax.dynamic_slice_in_dim(tile_users, start, TILE_DEV, 0)
        slots_item = lax.dynamic_slice_in_dim(tile_items, start, TILE_DEV, 0)
        local_steps = lax.dynamic_slice_in_dim(tile_steps, start, TILE_DEV, 0)
        ids_user = ((slots_user // CAP) * BLOCKS_DEV + asks_user[device][slots_user]).astype(jnp.int32)
        ids_item = ((slots_item // CAP) * BLOCKS_DEV + asks_item[device][slots_item]).astype(jnp.int32)
        steps = ((device // N_ROWS) * STEP_DEV + local_steps).astype(jnp.int32)
        left = user_factor[ids_user]
        right = item_factor[ids_item]
        cores = jnp.einsum('pqr,tr->tpq', core, time_factor[steps], precision=HIGH)
        live = (jnp.arange(TILE_DEV, dtype=jnp.int32) < tile_count[device]).astype(jnp.float32)
        mixed = jnp.einsum('tpq,tqj->tpj', cores, right, precision=HIGH)
        guess = jnp.einsum('tpi,tpj->tij', left, mixed, precision=HIGH)
        resid = (guess - values) * live[:, None, None]
        grad_u = jnp.einsum('tij,tpj->tpi', resid, mixed, precision=HIGH)
        across = jnp.einsum('tpi,tpq->tqi', left, cores, precision=HIGH)
        grad_v = jnp.einsum('tij,tqi->tqj', resid, across, precision=HIGH)
        inner = jnp.einsum('tpi,tij->tpj', left, resid, precision=HIGH)
        dcore = jnp.einsum('tpj,tqj->tpq', inner, right, precision=HIGH)
        grad_left = grad_left.at[ids_user].add(grad_u)
        grad_right = grad_right.at[ids_item].add(grad_v)
        step_sums = step_sums.at[steps].add(dcore)
        return (grad_left, grad_right, step_sums), None

    start_carry = (jnp.zeros((NB, RANK, BLOCK), jnp.float32), jnp.zeros((NB, RANK, BLOCK), jnp.float32), jnp.zeros((STEPS, RANK, RANK), jnp.float32))
    (grad_left, grad_right, step_sums), unused = lax.scan(visit, start_carry, jnp.arange(OWNERS, dtype=jnp.int32))
    grad_time = time_scale * jnp.einsum('spq,pqr->sr', step_sums, core, precision=HIGH)
    grad_core = core_scale * jnp.einsum('spq,sr->pqr', step_sums, time_factor, precision=HIGH)
    return (user_scale * grad_left, user_scale * grad_right, grad_time, grad_core)
```

```python
import functools

import jax
import jax.numpy as jnp
from jax import lax
from jax.experimental import pallas as pl
from jax.experimental.pallas import tpu as pltpu
from jax.sharding import PartitionSpec as P

HIGH = lax.Precision.HIGHEST
user_scale = 0.125
time_scale = 1.0 / 2048.0
core_scale = 1.0 / 4096.0
BOTH = ("tm", "rows")


def split(x):
    hi = x.astype(jnp.bfloat16)
    lo = (x - hi.astype(jnp.float32)).astype(jnp.bfloat16)
    return hi, lo


def split_outside(x):
    hi = lax.reduce_precision(x, 8, 7)
    return hi.astype(jnp.bfloat16), (x - hi).astype(jnp.bfloat16)


def mm(a, b):
    return jnp.dot(a, b, preferred_element_type=jnp.float32)


def tile_kernel(
    chunk, group, steps, rank,
    users, items, tsteps, count,
    values, left, right, c4, ct2, cq,
    out_u, out_v, out_d,
    u2, ut2, vt2, m2, psum, qsum,
):
    slots = left.shape[0]
    width = left.shape[2]
    step = pl.program_id(0)

    @pl.when(step == 0)
    def prepare():
        @pl.loop(0, slots)
        def one_slot(k):
            hi, lo = split(left[k])
            u2[k] = jnp.concatenate([hi, lo], 0)
            both = jnp.concatenate([hi.astype(jnp.float32), lo.astype(jnp.float32)], 0)
            ut2[k] = both.T.astype(jnp.bfloat16)
            hi, lo = split(right[k])
            both = jnp.concatenate([hi.astype(jnp.float32), lo.astype(jnp.float32)], 0)
            vt2[k] = both.T.astype(jnp.bfloat16)
            mixed = mm(c4[...], jnp.concatenate([hi, hi, lo, lo], 0))
            mhi, mlo = split(mixed)
            for s in range(steps):
                m2[k * steps + s, 0:rank, :] = mhi[s * rank:(s + 1) * rank]
                m2[k * steps + s, rank:2 * rank, :] = mlo[s * rank:(s + 1) * rank]
            psum[k] = jnp.zeros((steps * rank, width), jnp.float32)
            qsum[k] = jnp.zeros((width, steps * 2 * rank), jnp.float32)

    base = step * chunk
    live = jnp.clip(count[0] - base, 0, chunk)

    @pl.loop(0, (live + group - 1) // group)
    def one_group(g):
        first = g * group
        done = []
        for k in range(group):
            t = base + first + k
            u, v, s = users[t], items[t], tsteps[t]
            m = m2[v * steps + s]
            mhi, mlo = m[:rank], m[rank:]
            ut = ut2[u]
            guess = mm(
                jnp.concatenate([ut, ut], 1), jnp.concatenate([mhi, mhi, mlo, mlo], 0)
            )
            resid = guess - values[first + k].astype(jnp.float32)
            resid = jnp.where(first + k < live, resid, 0.0)
            rhi, rlo = split(resid)
            ul = u2[u]
            vt = vt2[v]
            w = mm(jnp.concatenate([ul, ul], 1), jnp.concatenate([rhi, rlo], 0))
            z = mm(jnp.concatenate([rhi, rlo], 1), jnp.concatenate([vt, vt], 0))
            done.append((u, v, s, w[:rank] + w[rank:], z))
        for u, v, s, w, z in done:
            at_p = pl.ds(pl.multiple_of(s * rank, rank), rank)
            psum[v, at_p, :] += w
            at_q = pl.ds(pl.multiple_of(s * 2 * rank, 2 * rank), 2 * rank)
            qsum[u, :, at_q] += z

    @pl.when(step == pl.num_programs(0) - 1)
    def finish():
        out_d[...] = jnp.zeros(out_d.shape, jnp.float32)

        @pl.loop(0, slots)
        def one_slot(k):
            hi, lo = split(psum[k])
            g1 = mm(ct2[...], hi)
            out_v[k] = g1[:rank] + g1[rank:] + mm(ct2[0:rank, :], lo)
            vt = vt2[k]
            out_d[...] += mm(
                jnp.concatenate([hi, lo], 1), jnp.concatenate([vt, vt], 0)
            )
            qhi, qlo = split(qsum[k])
            g2 = (mm(qhi, cq[...]) + mm(qlo, cq[...])).T
            out_u[k] = g2[:rank] + g2[rank:]


def tiles_in_kernel(values, users, items, tsteps, count, left, right, cores):
    slots, rank, width = left.shape
    steps = cores.shape[0]
    total = values.shape[0]
    chunk = 32
    group = 8
    chi, clo = split_outside(cores)
    flat_hi, flat_lo = chi.reshape(steps * rank, rank), clo.reshape(steps * rank, rank)
    c4 = jnp.concatenate([flat_hi, flat_lo, flat_hi, flat_lo], 1)
    ct2 = jnp.concatenate([flat_hi.T, flat_lo.T], 0)
    turned = jnp.concatenate([jnp.swapaxes(chi, 1, 2), jnp.swapaxes(clo, 1, 2)], 2)
    cq = jnp.concatenate([turned, turned], 1).reshape(steps * 2 * rank, 2 * rank)

    def values_at(i, users, items, tsteps, count):
        last = jnp.maximum((count[0] + chunk - 1) // chunk - 1, 0)
        return (jnp.minimum(i, last), 0, 0)

    whole = pl.BlockSpec(memory_space=pltpu.VMEM)
    return pl.pallas_call(
        functools.partial(tile_kernel, chunk, group, steps, rank),
        grid_spec=pltpu.PrefetchScalarGridSpec(
            num_scalar_prefetch=4,
            grid=(total // chunk,),
            in_specs=[pl.BlockSpec((chunk, width, width), values_at)] + [whole] * 5,
            out_specs=[whole] * 3,
            scratch_shapes=[
                pltpu.VMEM((slots, 2 * rank, width), jnp.bfloat16),
                pltpu.VMEM((slots, width, 2 * rank), jnp.bfloat16),
                pltpu.VMEM((slots, width, 2 * rank), jnp.bfloat16),
                pltpu.VMEM((slots * steps, 2 * rank, width), jnp.bfloat16),
                pltpu.VMEM((slots, steps * rank, width), jnp.float32),
                pltpu.VMEM((slots, width, steps * 2 * rank), jnp.float32),
            ],
        ),
        out_shape=[
            jax.ShapeDtypeStruct((slots, rank, width), jnp.float32),
            jax.ShapeDtypeStruct((slots, rank, width), jnp.float32),
            jax.ShapeDtypeStruct((steps * rank, 2 * rank), jnp.float32),
        ],
        compiler_params=pltpu.CompilerParams(
            dimension_semantics=("arbitrary",), vmem_limit_bytes=56 * 2**20
        ),
        name="tiles",
    )(users, items, tsteps, count, values, left, right, c4, ct2, cq)


def tiles_in_loop(values_all, users, items, tsteps, count, left_all, right_all, step_cores):
    slots, rank, width = left_all.shape
    step_count = step_cores.shape[0]
    block_size = min(64, values_all.shape[0])
    live_count = count[0]
    step_ids = jnp.arange(step_count, dtype=jnp.int32)

    def one_block(index, carry):
        grad_left, grad_right, step_sums = carry
        start = index * block_size
        values = lax.dynamic_slice_in_dim(values_all, start, block_size, 0).astype(jnp.float32)
        slots_user = lax.dynamic_slice_in_dim(users, start, block_size, 0)
        slots_item = lax.dynamic_slice_in_dim(items, start, block_size, 0)
        local_steps = lax.dynamic_slice_in_dim(tsteps, start, block_size, 0)
        picker = (local_steps[:, None] == step_ids[None, :]).astype(jnp.float32)
        cores = jnp.take(step_cores, local_steps, axis=0)
        left = jnp.take(left_all, slots_user, axis=0)
        right = jnp.take(right_all, slots_item, axis=0)
        live = (start + jnp.arange(block_size, dtype=jnp.int32) < live_count).astype(jnp.float32)
        mixed = jnp.einsum("tpq,tqj->tpj", cores, right, precision=HIGH)
        guess = jnp.einsum("tpi,tpj->tij", left, mixed, precision=HIGH)
        resid = (guess - values) * live[:, None, None]
        grad_u = jnp.einsum("tij,tpj->tpi", resid, mixed, precision=HIGH)
        across = jnp.einsum("tpi,tpq->tqi", left, cores, precision=HIGH)
        grad_v = jnp.einsum("tij,tqi->tqj", resid, across, precision=HIGH)
        inner = jnp.einsum("tpi,tij->tpj", left, resid, precision=HIGH)
        dcore = jnp.einsum("tpj,tqj->tpq", inner, right, precision=HIGH)
        grad_left = grad_left.at[slots_user].add(grad_u)
        grad_right = grad_right.at[slots_item].add(grad_v)
        step_sums = step_sums + jnp.einsum("ts,tpq->spq", picker, dcore, precision=HIGH)
        return (grad_left, grad_right, step_sums)

    carry = (
        jnp.zeros((slots, rank, width), jnp.float32),
        jnp.zeros((slots, rank, width), jnp.float32),
        jnp.zeros((step_count, rank, rank), jnp.float32),
    )
    return lax.fori_loop(0, (live_count + block_size - 1) // block_size, one_block, carry)


def shards(
    tile_values,
    tile_users,
    tile_items,
    tile_steps,
    tile_count,
    users_ask,
    items_ask,
    user_factor,
    item_factor,
    time_factor,
    core,
):
    count_tm = lax.axis_size("tm")
    count_rows = lax.axis_size("rows")
    owners = count_tm * count_rows
    cap = users_ask.shape[1]
    rank = user_factor.shape[1]
    width = user_factor.shape[2]
    blocks_own = user_factor.shape[0]
    steps = time_factor.shape[0]
    slots = owners * cap

    exchange = functools.partial(
        lax.all_to_all, axis_name=BOTH, split_axis=0, concat_axis=0, tiled=True
    )
    held = exchange(jnp.concatenate([users_ask, items_ask], 1))
    held_user, held_item = held[:, :cap], held[:, cap:]
    found = jnp.concatenate(
        [jnp.take(user_factor, held_user, axis=0), jnp.take(item_factor, held_item, axis=0)], 1
    )
    back = exchange(found)
    left = back[:, :cap].reshape(slots, rank, width)
    right = back[:, cap:].reshape(slots, rank, width)
    cores = jnp.einsum("pqr,sr->spq", core, time_factor, precision=HIGH)
    time_all = lax.all_gather(time_factor, "tm", axis=0, tiled=True)

    if slots <= 32 and tile_values.shape[0] % 32 == 0:
        part_u, part_v, twice = tiles_in_kernel(
            tile_values, tile_users, tile_items, tile_steps, tile_count, left, right, cores
        )
        step_sums = (twice[:, :rank] + twice[:, rank:]).reshape(steps, rank, rank)
    else:
        part_u, part_v, step_sums = tiles_in_loop(
            tile_values, tile_users, tile_items, tile_steps, tile_count, left, right, cores
        )

    own_steps = lax.psum_scatter(
        step_sums.reshape(steps * rank * rank // 128, 128), "rows", scatter_dimension=0, tiled=True
    )
    every = lax.all_gather(own_steps, BOTH, axis=0, tiled=True)
    every = every.reshape(count_tm * steps, rank, rank)
    returned = exchange(
        jnp.concatenate(
            [part_u.reshape(owners, cap, rank, width), part_v.reshape(owners, cap, rank, width)], 1
        )
    )
    own_ids = jnp.arange(blocks_own, dtype=jnp.int32)

    def to_owner(ids, terms):
        pick = (ids.reshape(slots)[:, None] == own_ids[None, :]).astype(jnp.float32)
        return user_scale * jnp.einsum(
            "nb,npi->bpi", pick, terms.reshape(slots, rank, width), precision=HIGH
        )

    grad_users = to_owner(held_user, returned[:, :cap])
    grad_items = to_owner(held_item, returned[:, cap:])
    mine = lax.dynamic_slice_in_dim(every, lax.axis_index("tm") * steps, steps, 0)
    grad_time = time_scale * jnp.einsum("spq,pqr->sr", mine, core, precision=HIGH)
    grad_core = core_scale * jnp.einsum("spq,sr->pqr", every, time_all, precision=HIGH)
    return (grad_users, grad_items, grad_time, grad_core)


def solution(mesh):
    in_specs = (
        P(BOTH, None, None),
        P(BOTH),
        P(BOTH),
        P(BOTH),
        P(BOTH),
        P(BOTH, None),
        P(BOTH, None),
        P(BOTH, None, None),
        P(BOTH, None, None),
        P("tm", None),
        P(),
    )
    out_specs = (P(BOTH, None, None), P(BOTH, None, None), P("tm", None), P())
    return jax.shard_map(shards, mesh=mesh, in_specs=in_specs, out_specs=out_specs, check_vma=False)
```

```python
import functools

import jax
import jax.numpy as jnp
from jax import lax
from jax.experimental import pallas as pl
from jax.experimental.pallas import tpu as pltpu
from jax.sharding import PartitionSpec as P

HIGH = lax.Precision.HIGHEST
user_scale = 0.125
time_scale = 1.0 / 2048.0
core_scale = 1.0 / 4096.0
BOTH = ("tm", "rows")


def split(x):
    hi = x.astype(jnp.bfloat16)
    lo = (x - hi.astype(jnp.float32)).astype(jnp.bfloat16)
    return hi, lo


def split_outside(x):
    hi = lax.reduce_precision(x, 8, 7)
    return hi.astype(jnp.bfloat16), (x - hi).astype(jnp.bfloat16)


def mm(a, b):
    return jnp.dot(a, b, preferred_element_type=jnp.float32)


def tile_kernel(
    chunk, group, ahead, steps, rank,
    users, items, tsteps, count,
    values, blocks, c4, ct2, cq,
    out, out_d,
    u2, ut2, vt2, m2, psum, qsum,
):
    slots = blocks.shape[0]
    width = blocks.shape[3]
    step = pl.program_id(0)

    @pl.when(step == 0)
    def prepare():
        def one_slot(k, carry):
            hi, lo = split(blocks[k, 0])
            u2[k] = jnp.concatenate([hi, lo], 0)
            both = jnp.concatenate([hi.astype(jnp.float32), lo.astype(jnp.float32)], 0)
            ut2[k] = both.T.astype(jnp.bfloat16)
            hi, lo = split(blocks[k, 1])
            both = jnp.concatenate([hi.astype(jnp.float32), lo.astype(jnp.float32)], 0)
            vt2[k] = both.T.astype(jnp.bfloat16)
            mixed = mm(c4[...], jnp.concatenate([hi, hi, lo, lo], 0))
            mhi, mlo = split(mixed)
            for s in range(steps):
                m2[k * steps + s, 0:rank, :] = mhi[s * rank:(s + 1) * rank]
                m2[k * steps + s, rank:2 * rank, :] = mlo[s * rank:(s + 1) * rank]
            psum[k] = jnp.zeros((steps * rank, width), jnp.float32)
            qsum[k] = jnp.zeros((width, steps * 2 * rank), jnp.float32)
            return carry

        lax.fori_loop(0, slots, one_slot, 0, unroll=2)

    base = step * chunk
    live = jnp.clip(count[0] - base, 0, chunk)

    @pl.loop(0, (live + group - 1) // group)
    def one_group(g):
        first = g * group
        ids = []
        for k in range(group):
            t = base + first + k
            ids.append((users[t], items[t], tsteps[t]))

        def guess_of(k):
            u, v, s = ids[k]
            m = m2[v * steps + s]
            mhi, mlo = m[:rank], m[rank:]
            ut = ut2[u]
            return mm(
                jnp.concatenate([ut, ut], 1), jnp.concatenate([mhi, mhi, mlo, mlo], 0)
            )

        def products_of(k, guess):
            u, v, s = ids[k]
            resid = guess - values[first + k].astype(jnp.float32)
            resid = jnp.where(first + k < live, resid, 0.0)
            rhi, rlo = split(resid)
            ul = u2[u]
            vt = vt2[v]
            w = mm(jnp.concatenate([ul, ul], 1), jnp.concatenate([rhi, rlo], 0))
            z = mm(jnp.concatenate([rhi, rlo], 1), jnp.concatenate([vt, vt], 0))
            return w[:rank] + w[rank:], z

        def add_up(k, w, z):
            u, v, s = ids[k]
            at_p = pl.ds(pl.multiple_of(s * rank, rank), rank)
            psum[v, at_p, :] += w
            at_q = pl.ds(pl.multiple_of(s * 2 * rank, 2 * rank), 2 * rank)
            qsum[u, :, at_q] += z

        guesses, products = {}, {}
        for k in range(group + ahead + 2):
            if k < group:
                guesses[k] = guess_of(k)
            if 0 <= k - ahead < group:
                products[k - ahead] = products_of(k - ahead, guesses.pop(k - ahead))
            if 0 <= k - ahead - 2 < group:
                add_up(k - ahead - 2, *products.pop(k - ahead - 2))

    @pl.when(step == pl.num_programs(0) - 1)
    def finish():
        out_d[...] = jnp.zeros(out_d.shape, jnp.float32)

        def one_slot(k, carry):
            hi, lo = split(psum[k])
            g1 = mm(ct2[...], hi)
            out[k, 1] = g1[:rank] + g1[rank:] + mm(ct2[0:rank, :], lo)
            vt = vt2[k]
            out_d[...] += mm(
                jnp.concatenate([hi, lo], 1), jnp.concatenate([vt, vt], 0)
            )
            qhi, qlo = split(qsum[k])
            g2 = (mm(qhi, cq[...]) + mm(qlo, cq[...])).T
            out[k, 0] = g2[:rank] + g2[rank:]
            return carry

        lax.fori_loop(0, slots, one_slot, 0, unroll=2)


def tiles_in_kernel(values, users, items, tsteps, count, blocks, cores):
    slots, unused, rank, width = blocks.shape
    steps = cores.shape[0]
    total = values.shape[0]
    chunk = 32
    group = 16
    ahead = 4
    chi, clo = split_outside(cores)
    flat_hi, flat_lo = chi.reshape(steps * rank, rank), clo.reshape(steps * rank, rank)
    c4 = jnp.concatenate([flat_hi, flat_lo, flat_hi, flat_lo], 1)
    ct2 = jnp.concatenate([flat_hi.T, flat_lo.T], 0)
    turned = jnp.concatenate([jnp.swapaxes(chi, 1, 2), jnp.swapaxes(clo, 1, 2)], 2)
    cq = jnp.concatenate([turned, turned], 1).reshape(steps * 2 * rank, 2 * rank)

    def values_at(i, users, items, tsteps, count):
        last = jnp.maximum((count[0] + chunk - 1) // chunk - 1, 0)
        return (jnp.minimum(i, last), 0, 0)

    whole = pl.BlockSpec(memory_space=pltpu.VMEM)
    return pl.pallas_call(
        functools.partial(tile_kernel, chunk, group, ahead, steps, rank),
        grid_spec=pltpu.PrefetchScalarGridSpec(
            num_scalar_prefetch=4,
            grid=(total // chunk,),
            in_specs=[pl.BlockSpec((chunk, width, width), values_at)] + [whole] * 4,
            out_specs=[whole] * 2,
            scratch_shapes=[
                pltpu.VMEM((slots, 2 * rank, width), jnp.bfloat16),
                pltpu.VMEM((slots, width, 2 * rank), jnp.bfloat16),
                pltpu.VMEM((slots, width, 2 * rank), jnp.bfloat16),
                pltpu.VMEM((slots * steps, 2 * rank, width), jnp.bfloat16),
                pltpu.VMEM((slots, steps * rank, width), jnp.float32),
                pltpu.VMEM((slots, width, steps * 2 * rank), jnp.float32),
            ],
        ),
        out_shape=[
            jax.ShapeDtypeStruct(blocks.shape, jnp.float32),
            jax.ShapeDtypeStruct((steps * rank, 2 * rank), jnp.float32),
        ],
        compiler_params=pltpu.CompilerParams(
            dimension_semantics=("arbitrary",), vmem_limit_bytes=56 * 2**20
        ),
        name="tiles",
    )(users, items, tsteps, count, values, blocks, c4, ct2, cq)


def pick_kernel(held, left, right, out):
    cap = held.shape[1] // 2

    @pl.loop(0, held.shape[0])
    def one_owner(k):
        for c in range(cap):
            out[k, c] = left[held[k, c]]
            out[k, cap + c] = right[held[k, cap + c]]


def owner_kernel(held, terms, out_left, out_right):
    cap = held.shape[1] // 2
    out_left[...] = jnp.zeros(out_left.shape, jnp.float32)
    out_right[...] = jnp.zeros(out_right.shape, jnp.float32)

    @pl.loop(0, held.shape[0])
    def one_owner(k):
        for c in range(cap):
            out_left[held[k, c]] += user_scale * terms[k, c]
            out_right[held[k, cap + c]] += user_scale * terms[k, cap + c]


def plain_kernel(body, shapes, held, *arrays, name):
    whole = pl.BlockSpec(memory_space=pltpu.VMEM)
    return pl.pallas_call(
        body,
        in_specs=[pl.BlockSpec(memory_space=pltpu.SMEM)] + [whole] * len(arrays),
        out_specs=[whole] * len(shapes),
        out_shape=[jax.ShapeDtypeStruct(shape, jnp.float32) for shape in shapes],
        compiler_params=pltpu.CompilerParams(vmem_limit_bytes=32 * 2**20),
        name=name,
    )(held, *arrays)


def tiles_in_loop(values_all, users, items, tsteps, count, left_all, right_all, step_cores):
    slots, rank, width = left_all.shape
    step_count = step_cores.shape[0]
    block_size = min(64, values_all.shape[0])
    live_count = count[0]
    step_ids = jnp.arange(step_count, dtype=jnp.int32)

    def one_block(index, carry):
        grad_left, grad_right, step_sums = carry
        start = index * block_size
        values = lax.dynamic_slice_in_dim(values_all, start, block_size, 0).astype(jnp.float32)
        slots_user = lax.dynamic_slice_in_dim(users, start, block_size, 0)
        slots_item = lax.dynamic_slice_in_dim(items, start, block_size, 0)
        local_steps = lax.dynamic_slice_in_dim(tsteps, start, block_size, 0)
        picker = (local_steps[:, None] == step_ids[None, :]).astype(jnp.float32)
        cores = jnp.take(step_cores, local_steps, axis=0)
        left = jnp.take(left_all, slots_user, axis=0)
        right = jnp.take(right_all, slots_item, axis=0)
        live = (start + jnp.arange(block_size, dtype=jnp.int32) < live_count).astype(jnp.float32)
        mixed = jnp.einsum("tpq,tqj->tpj", cores, right, precision=HIGH)
        guess = jnp.einsum("tpi,tpj->tij", left, mixed, precision=HIGH)
        resid = (guess - values) * live[:, None, None]
        grad_u = jnp.einsum("tij,tpj->tpi", resid, mixed, precision=HIGH)
        across = jnp.einsum("tpi,tpq->tqi", left, cores, precision=HIGH)
        grad_v = jnp.einsum("tij,tqi->tqj", resid, across, precision=HIGH)
        inner = jnp.einsum("tpi,tij->tpj", left, resid, precision=HIGH)
        dcore = jnp.einsum("tpj,tqj->tpq", inner, right, precision=HIGH)
        grad_left = grad_left.at[slots_user].add(grad_u)
        grad_right = grad_right.at[slots_item].add(grad_v)
        step_sums = step_sums + jnp.einsum("ts,tpq->spq", picker, dcore, precision=HIGH)
        return (grad_left, grad_right, step_sums)

    carry = (
        jnp.zeros((slots, rank, width), jnp.float32),
        jnp.zeros((slots, rank, width), jnp.float32),
        jnp.zeros((step_count, rank, rank), jnp.float32),
    )
    return lax.fori_loop(0, (live_count + block_size - 1) // block_size, one_block, carry)


def shards(
    tile_values,
    tile_users,
    tile_items,
    tile_steps,
    tile_count,
    users_ask,
    items_ask,
    user_factor,
    item_factor,
    time_factor,
    core,
):
    count_tm = lax.axis_size("tm")
    count_rows = lax.axis_size("rows")
    owners = count_tm * count_rows
    cap = users_ask.shape[1]
    rank = user_factor.shape[1]
    width = user_factor.shape[2]
    steps = time_factor.shape[0]
    slots = owners * cap

    exchange = functools.partial(
        lax.all_to_all, axis_name=BOTH, split_axis=0, concat_axis=0, tiled=True
    )
    held = exchange(jnp.concatenate([users_ask, items_ask], 1))
    (found,) = plain_kernel(
        pick_kernel,
        [(owners, 2 * cap, rank, width)],
        held,
        user_factor,
        item_factor,
        name="pick",
    )
    back = exchange(found)
    cores = jnp.einsum("pqr,sr->spq", core, time_factor, precision=HIGH)

    if slots <= 32 and cap == 1 and tile_values.shape[0] % 32 == 0:
        terms, twice = tiles_in_kernel(
            tile_values, tile_users, tile_items, tile_steps, tile_count, back, cores
        )
        step_sums = twice[:, :rank] + twice[:, rank:]
    else:
        left = back[:, :cap].reshape(slots, rank, width)
        right = back[:, cap:].reshape(slots, rank, width)
        part_u, part_v, step_sums = tiles_in_loop(
            tile_values, tile_users, tile_items, tile_steps, tile_count, left, right, cores
        )
        terms = jnp.concatenate(
            [part_u.reshape(owners, cap, rank, width), part_v.reshape(owners, cap, rank, width)], 1
        )

    own_steps = lax.psum_scatter(
        step_sums.reshape(steps * rank * rank // 128, 128), "rows", scatter_dimension=0, tiled=True
    )
    share = steps // count_rows
    own_time = lax.dynamic_slice_in_dim(time_factor, lax.axis_index("rows") * share, share, 0)
    own_time = jnp.pad(own_time.reshape(-1), (0, 8 * 128 - share * rank)).reshape(8, 128)
    every = lax.all_gather(jnp.concatenate([own_steps, own_time], 0), BOTH, axis=0)
    time_all = every[:, -8:].reshape(owners, 8 * 128)[:, : share * rank]
    time_all = time_all.reshape(count_tm * steps, rank)
    every = every[:, :-8].reshape(count_tm * steps, rank, rank)
    returned = exchange(terms)
    grad_users, grad_items = plain_kernel(
        owner_kernel, [user_factor.shape, item_factor.shape], held, returned, name="owner_sums"
    )
    mine = lax.dynamic_slice_in_dim(every, lax.axis_index("tm") * steps, steps, 0)
    grad_time = time_scale * jnp.einsum("spq,pqr->sr", mine, core, precision=HIGH)
    grad_core = core_scale * jnp.einsum("spq,sr->pqr", every, time_all, precision=HIGH)
    return (grad_users, grad_items, grad_time, grad_core)


def solution(mesh):
    in_specs = (
        P(BOTH, None, None),
        P(BOTH),
        P(BOTH),
        P(BOTH),
        P(BOTH),
        P(BOTH, None),
        P(BOTH, None),
        P(BOTH, None, None),
        P(BOTH, None, None),
        P("tm", None),
        P(),
    )
    out_specs = (P(BOTH, None, None), P(BOTH, None, None), P("tm", None), P())
    return jax.shard_map(shards, mesh=mesh, in_specs=in_specs, out_specs=out_specs, check_vma=False)
```

```python
import functools

import jax
import jax.numpy as jnp
from jax import lax
from jax.experimental import pallas as pl
from jax.experimental.pallas import tpu as pltpu
from jax.sharding import PartitionSpec as P

HIGH = lax.Precision.HIGHEST
user_scale = 0.125
time_scale = 1.0 / 2048.0
core_scale = 1.0 / 4096.0
BOTH = ("tm", "rows")


def split(x):
    hi = x.astype(jnp.bfloat16)
    lo = (x - hi.astype(jnp.float32)).astype(jnp.bfloat16)
    return hi, lo


def split_outside(x):
    hi = lax.reduce_precision(x, 8, 7)
    return hi.astype(jnp.bfloat16), (x - hi).astype(jnp.bfloat16)


def mm(a, b):
    return jnp.dot(a, b, preferred_element_type=jnp.float32)


def tile_kernel(
    chunk, group, ahead, steps, rank,
    users, items, tsteps, count,
    values, blocks, c4, ct2, cq,
    out, out_d,
    u2, ut2, vt2, m2, psum, qsum,
):
    slots = blocks.shape[0]
    width = blocks.shape[3]
    step = pl.program_id(0)

    @pl.when(step == 0)
    def prepare():
        def one_slot(k, carry):
            hi, lo = split(blocks[k, 0])
            u2[k] = jnp.concatenate([hi, lo], 0)
            both = jnp.concatenate([hi.astype(jnp.float32), lo.astype(jnp.float32)], 0)
            ut2[k] = both.T.astype(jnp.bfloat16)
            hi, lo = split(blocks[k, 1])
            both = jnp.concatenate([hi.astype(jnp.float32), lo.astype(jnp.float32)], 0)
            vt2[k] = both.T.astype(jnp.bfloat16)
            mixed = mm(c4[...], jnp.concatenate([hi, hi, lo, lo], 0))
            mhi, mlo = split(mixed)
            for s in range(steps):
                m2[k * steps + s, 0:rank, :] = mhi[s * rank:(s + 1) * rank]
                m2[k * steps + s, rank:2 * rank, :] = mlo[s * rank:(s + 1) * rank]
            psum[k] = jnp.zeros((steps * rank, width), jnp.float32)
            qsum[k] = jnp.zeros((width, steps * 2 * rank), jnp.float32)
            return carry

        lax.fori_loop(0, slots, one_slot, 0, unroll=2)

    base = step * chunk
    live = jnp.clip(count[0] - base, 0, chunk)

    @pl.loop(0, (live + group - 1) // group)
    def one_group(g):
        first = g * group
        ids = []
        for k in range(group):
            t = base + first + k
            ids.append((users[t], items[t], tsteps[t]))

        def guess_of(k):
            u, v, s = ids[k]
            m = m2[v * steps + s]
            mhi, mlo = m[:rank], m[rank:]
            ut = ut2[u]
            return mm(
                jnp.concatenate([ut, ut], 1), jnp.concatenate([mhi, mhi, mlo, mlo], 0)
            )

        def products_of(k, guess):
            u, v, s = ids[k]
            resid = guess - values[first + k].astype(jnp.float32)
            resid = jnp.where(first + k < live, resid, 0.0)
            rhi, rlo = split(resid)
            ul = u2[u]
            vt = vt2[v]
            w = mm(jnp.concatenate([ul, ul], 1), jnp.concatenate([rhi, rlo], 0))
            z = mm(jnp.concatenate([rhi, rlo], 1), jnp.concatenate([vt, vt], 0))
            return w[:rank] + w[rank:], z

        def add_up(k, w, z):
            u, v, s = ids[k]
            at_p = pl.ds(pl.multiple_of(s * rank, rank), rank)
            psum[v, at_p, :] += w
            at_q = pl.ds(pl.multiple_of(s * 2 * rank, 2 * rank), 2 * rank)
            qsum[u, :, at_q] += z

        guesses, products = {}, {}
        for k in range(group + ahead + 2):
            if k < group:
                guesses[k] = guess_of(k)
            if 0 <= k - ahead < group:
                products[k - ahead] = products_of(k - ahead, guesses.pop(k - ahead))
            if 0 <= k - ahead - 2 < group:
                add_up(k - ahead - 2, *products.pop(k - ahead - 2))

    @pl.when(step == pl.num_programs(0) - 1)
    def finish():
        out_d[...] = jnp.zeros(out_d.shape, jnp.float32)

        def one_slot(k, carry):
            hi, lo = split(psum[k])
            g1 = mm(ct2[...], hi)
            out[k, 1] = g1[:rank] + g1[rank:] + mm(ct2[0:rank, :], lo)
            vt = vt2[k]
            out_d[...] += mm(
                jnp.concatenate([hi, lo], 1), jnp.concatenate([vt, vt], 0)
            )
            qhi, qlo = split(qsum[k])
            g2 = (mm(qhi, cq[...]) + mm(qlo, cq[...])).T
            out[k, 0] = g2[:rank] + g2[rank:]
            return carry

        lax.fori_loop(0, slots, one_slot, 0, unroll=2)


def tiles_in_kernel(values, users, items, tsteps, count, blocks, cores):
    slots, unused, rank, width = blocks.shape
    steps = cores.shape[0]
    total = values.shape[0]
    chunk = 64
    group = 16
    ahead = 4
    chi, clo = split_outside(cores)
    flat_hi, flat_lo = chi.reshape(steps * rank, rank), clo.reshape(steps * rank, rank)
    c4 = jnp.concatenate([flat_hi, flat_lo, flat_hi, flat_lo], 1)
    ct2 = jnp.concatenate([flat_hi.T, flat_lo.T], 0)
    turned = jnp.concatenate([jnp.swapaxes(chi, 1, 2), jnp.swapaxes(clo, 1, 2)], 2)
    cq = jnp.concatenate([turned, turned], 1).reshape(steps * 2 * rank, 2 * rank)

    def values_at(i, users, items, tsteps, count):
        last = jnp.maximum((count[0] + chunk - 1) // chunk - 1, 0)
        return (jnp.minimum(i, last), 0, 0)

    whole = pl.BlockSpec(memory_space=pltpu.VMEM)
    return pl.pallas_call(
        functools.partial(tile_kernel, chunk, group, ahead, steps, rank),
        grid_spec=pltpu.PrefetchScalarGridSpec(
            num_scalar_prefetch=4,
            grid=(total // chunk,),
            in_specs=[pl.BlockSpec((chunk, width, width), values_at)] + [whole] * 4,
            out_specs=[whole] * 2,
            scratch_shapes=[
                pltpu.VMEM((slots, 2 * rank, width), jnp.bfloat16),
                pltpu.VMEM((slots, width, 2 * rank), jnp.bfloat16),
                pltpu.VMEM((slots, width, 2 * rank), jnp.bfloat16),
                pltpu.VMEM((slots * steps, 2 * rank, width), jnp.bfloat16),
                pltpu.VMEM((slots, steps * rank, width), jnp.float32),
                pltpu.VMEM((slots, width, steps * 2 * rank), jnp.float32),
            ],
        ),
        out_shape=[
            jax.ShapeDtypeStruct(blocks.shape, jnp.float32),
            jax.ShapeDtypeStruct((steps * rank, 2 * rank), jnp.float32),
        ],
        compiler_params=pltpu.CompilerParams(
            dimension_semantics=("arbitrary",), vmem_limit_bytes=56 * 2**20
        ),
        name="tiles",
    )(users, items, tsteps, count, values, blocks, c4, ct2, cq)


def pick_kernel(held, left, right, out):
    cap = held.shape[1] // 2

    @pl.loop(0, held.shape[0])
    def one_owner(k):
        for c in range(cap):
            out[k, c] = left[held[k, c]]
            out[k, cap + c] = right[held[k, cap + c]]


def owner_kernel(held, terms, out_left, out_right):
    cap = held.shape[1] // 2
    out_left[...] = jnp.zeros(out_left.shape, jnp.float32)
    out_right[...] = jnp.zeros(out_right.shape, jnp.float32)

    @pl.loop(0, held.shape[0])
    def one_owner(k):
        for c in range(cap):
            out_left[held[k, c]] += user_scale * terms[k, c]
            out_right[held[k, cap + c]] += user_scale * terms[k, cap + c]


def plain_kernel(body, shapes, held, *arrays, name):
    whole = pl.BlockSpec(memory_space=pltpu.VMEM)
    return pl.pallas_call(
        body,
        in_specs=[pl.BlockSpec(memory_space=pltpu.SMEM)] + [whole] * len(arrays),
        out_specs=[whole] * len(shapes),
        out_shape=[jax.ShapeDtypeStruct(shape, jnp.float32) for shape in shapes],
        compiler_params=pltpu.CompilerParams(vmem_limit_bytes=32 * 2**20),
        name=name,
    )(held, *arrays)


def tiles_in_loop(values_all, users, items, tsteps, count, left_all, right_all, step_cores):
    slots, rank, width = left_all.shape
    step_count = step_cores.shape[0]
    block_size = min(64, values_all.shape[0])
    live_count = count[0]
    step_ids = jnp.arange(step_count, dtype=jnp.int32)

    def one_block(index, carry):
        grad_left, grad_right, step_sums = carry
        start = index * block_size
        values = lax.dynamic_slice_in_dim(values_all, start, block_size, 0).astype(jnp.float32)
        slots_user = lax.dynamic_slice_in_dim(users, start, block_size, 0)
        slots_item = lax.dynamic_slice_in_dim(items, start, block_size, 0)
        local_steps = lax.dynamic_slice_in_dim(tsteps, start, block_size, 0)
        picker = (local_steps[:, None] == step_ids[None, :]).astype(jnp.float32)
        cores = jnp.take(step_cores, local_steps, axis=0)
        left = jnp.take(left_all, slots_user, axis=0)
        right = jnp.take(right_all, slots_item, axis=0)
        live = (start + jnp.arange(block_size, dtype=jnp.int32) < live_count).astype(jnp.float32)
        mixed = jnp.einsum("tpq,tqj->tpj", cores, right, precision=HIGH)
        guess = jnp.einsum("tpi,tpj->tij", left, mixed, precision=HIGH)
        resid = (guess - values) * live[:, None, None]
        grad_u = jnp.einsum("tij,tpj->tpi", resid, mixed, precision=HIGH)
        across = jnp.einsum("tpi,tpq->tqi", left, cores, precision=HIGH)
        grad_v = jnp.einsum("tij,tqi->tqj", resid, across, precision=HIGH)
        inner = jnp.einsum("tpi,tij->tpj", left, resid, precision=HIGH)
        dcore = jnp.einsum("tpj,tqj->tpq", inner, right, precision=HIGH)
        grad_left = grad_left.at[slots_user].add(grad_u)
        grad_right = grad_right.at[slots_item].add(grad_v)
        step_sums = step_sums + jnp.einsum("ts,tpq->spq", picker, dcore, precision=HIGH)
        return (grad_left, grad_right, step_sums)

    carry = (
        jnp.zeros((slots, rank, width), jnp.float32),
        jnp.zeros((slots, rank, width), jnp.float32),
        jnp.zeros((step_count, rank, rank), jnp.float32),
    )
    return lax.fori_loop(0, (live_count + block_size - 1) // block_size, one_block, carry)


def spread(x, axis, count):
    return lax.all_to_all(
        jnp.broadcast_to(x[None], (count,) + x.shape), axis, split_axis=0, concat_axis=0, tiled=True
    )


def shards(
    tile_values,
    tile_users,
    tile_items,
    tile_steps,
    tile_count,
    users_ask,
    items_ask,
    user_factor,
    item_factor,
    time_factor,
    core,
):
    count_tm = lax.axis_size("tm")
    count_rows = lax.axis_size("rows")
    owners = count_tm * count_rows
    cap = users_ask.shape[1]
    rank = user_factor.shape[1]
    width = user_factor.shape[2]
    steps = time_factor.shape[0]
    slots = owners * cap

    exchange = functools.partial(
        lax.all_to_all, axis_name=BOTH, split_axis=0, concat_axis=0, tiled=True
    )
    held = exchange(jnp.concatenate([users_ask, items_ask], 1))
    (found,) = plain_kernel(
        pick_kernel,
        [(owners, 2 * cap, rank, width)],
        held,
        user_factor,
        item_factor,
        name="pick",
    )
    back = exchange(found)
    cores = jnp.einsum("pqr,sr->spq", core, time_factor, precision=HIGH)

    if slots <= 32 and cap == 1 and tile_values.shape[0] % 64 == 0:
        terms, twice = tiles_in_kernel(
            tile_values, tile_users, tile_items, tile_steps, tile_count, back, cores
        )
        step_sums = twice[:, :rank] + twice[:, rank:]
    else:
        left = back[:, :cap].reshape(slots, rank, width)
        right = back[:, cap:].reshape(slots, rank, width)
        part_u, part_v, step_sums = tiles_in_loop(
            tile_values, tile_users, tile_items, tile_steps, tile_count, left, right, cores
        )
        terms = jnp.concatenate(
            [part_u.reshape(owners, cap, rank, width), part_v.reshape(owners, cap, rank, width)], 1
        )

    share = steps // count_rows
    lanes = share * rank * rank // 128
    own_steps = lax.all_to_all(
        step_sums.reshape(count_rows, lanes, 128), "rows", split_axis=0, concat_axis=0, tiled=True
    ).sum(0)
    own_time = lax.dynamic_slice_in_dim(time_factor, lax.axis_index("rows") * share, share, 0)
    own_time = jnp.pad(own_time.reshape(-1), (0, 8 * 128 - share * rank)).reshape(8, 128)
    piece = jnp.concatenate([own_steps, own_time], 0)
    over_tm = spread(piece, "tm", count_tm)
    terms, over_tm = lax.optimization_barrier((terms, over_tm))
    returned = exchange(terms)
    every = spread(over_tm, "rows", count_rows)
    time_all = every[:, :, lanes:].reshape(owners, 8 * 128)[:, : share * rank]
    time_all = time_all.reshape(owners * share, rank)
    mine = lax.dynamic_index_in_dim(every, lax.axis_index("tm"), 1, keepdims=False)
    mine = mine[:, :lanes].reshape(steps, rank, rank)
    every = every[:, :, :lanes].reshape(owners * share, rank, rank)
    grad_users, grad_items = plain_kernel(
        owner_kernel, [user_factor.shape, item_factor.shape], held, returned, name="owner_sums"
    )
    grad_time = time_scale * jnp.einsum("spq,pqr->sr", mine, core, precision=HIGH)
    grad_core = core_scale * jnp.einsum("spq,sr->pqr", every, time_all, precision=HIGH)
    return (grad_users, grad_items, grad_time, grad_core)


def solution(mesh):
    in_specs = (
        P(BOTH, None, None),
        P(BOTH),
        P(BOTH),
        P(BOTH),
        P(BOTH),
        P(BOTH, None),
        P(BOTH, None),
        P(BOTH, None, None),
        P(BOTH, None, None),
        P("tm", None),
        P(),
    )
    out_specs = (P(BOTH, None, None), P(BOTH, None, None), P("tm", None), P())
    return jax.shard_map(shards, mesh=mesh, in_specs=in_specs, out_specs=out_specs, check_vma=False)
```

```python
import functools

import jax
import jax.numpy as jnp
from jax import lax
from jax.experimental import pallas as pl
from jax.experimental.pallas import tpu as pltpu
from jax.sharding import PartitionSpec as P

HIGH = lax.Precision.HIGHEST
user_scale = 0.125
time_scale = 1.0 / 2048.0
core_scale = 1.0 / 4096.0
BOTH = ("tm", "rows")


def split(x):
    hi = x.astype(jnp.bfloat16)
    lo = (x - hi.astype(jnp.float32)).astype(jnp.bfloat16)
    return hi, lo


def split_outside(x):
    hi = lax.reduce_precision(x, 8, 7)
    return hi.astype(jnp.bfloat16), (x - hi).astype(jnp.bfloat16)


def mm(a, b):
    return jnp.dot(a, b, preferred_element_type=jnp.float32)


def tile_kernel(
    chunk, group, ahead, steps, rank,
    users, items, tsteps, count,
    values, blocks, c4, ct2, cq,
    out_u, out_v, out_d,
    u2, ut2, vt2, m2, psum, qsum,
):
    slots = blocks.shape[0]
    width = blocks.shape[3]
    step = pl.program_id(0)

    @pl.when(step == 0)
    def prepare():
        def one_slot(k, carry):
            hi, lo = split(blocks[k, 0])
            u2[k] = jnp.concatenate([hi, lo], 0)
            both = jnp.concatenate([hi.astype(jnp.float32), lo.astype(jnp.float32)], 0)
            ut2[k] = both.T.astype(jnp.bfloat16)
            hi, lo = split(blocks[k, 1])
            both = jnp.concatenate([hi.astype(jnp.float32), lo.astype(jnp.float32)], 0)
            vt2[k] = both.T.astype(jnp.bfloat16)
            mixed = mm(c4[...], jnp.concatenate([hi, hi, lo, lo], 0))
            mhi, mlo = split(mixed)
            for s in range(steps):
                m2[k * steps + s, 0:rank, :] = mhi[s * rank:(s + 1) * rank]
                m2[k * steps + s, rank:2 * rank, :] = mlo[s * rank:(s + 1) * rank]
            psum[k] = jnp.zeros((steps * rank, width), jnp.float32)
            qsum[k] = jnp.zeros((width, steps * 2 * rank), jnp.float32)
            return carry

        lax.fori_loop(0, slots, one_slot, 0, unroll=2)

    base = step * chunk
    live = jnp.clip(count[0] - base, 0, chunk)

    @pl.loop(0, (live + group - 1) // group)
    def one_group(g):
        first = g * group
        ids = []
        for k in range(group):
            t = base + first + k
            ids.append((users[t], items[t], tsteps[t]))

        def guess_of(k):
            u, v, s = ids[k]
            m = m2[v * steps + s]
            mhi, mlo = m[:rank], m[rank:]
            ut = ut2[u]
            return mm(
                jnp.concatenate([ut, ut], 1), jnp.concatenate([mhi, mhi, mlo, mlo], 0)
            )

        def products_of(k, guess):
            u, v, s = ids[k]
            resid = guess - values[first + k].astype(jnp.float32)
            resid = jnp.where(first + k < live, resid, 0.0)
            rhi, rlo = split(resid)
            ul = u2[u]
            vt = vt2[v]
            w = mm(jnp.concatenate([ul, ul], 1), jnp.concatenate([rhi, rlo], 0))
            z = mm(jnp.concatenate([rhi, rlo], 1), jnp.concatenate([vt, vt], 0))
            return w[:rank] + w[rank:], z

        def add_up(k, w, z):
            u, v, s = ids[k]
            at_p = pl.ds(pl.multiple_of(s * rank, rank), rank)
            psum[v, at_p, :] += w
            at_q = pl.ds(pl.multiple_of(s * 2 * rank, 2 * rank), 2 * rank)
            qsum[u, :, at_q] += z

        guesses, products = {}, {}
        for k in range(group + ahead + 2):
            if k < group:
                guesses[k] = guess_of(k)
            if 0 <= k - ahead < group:
                products[k - ahead] = products_of(k - ahead, guesses.pop(k - ahead))
            if 0 <= k - ahead - 2 < group:
                add_up(k - ahead - 2, *products.pop(k - ahead - 2))

    @pl.when(step == pl.num_programs(0) - 1)
    def finish():
        out_d[...] = jnp.zeros(out_d.shape, jnp.float32)

        def one_slot(k, carry):
            hi, lo = split(psum[k])
            g1 = mm(ct2[...], hi)
            out_v[k, 0] = g1[:rank] + g1[rank:] + mm(ct2[0:rank, :], lo)
            vt = vt2[k]
            out_d[...] += mm(
                jnp.concatenate([hi, lo], 1), jnp.concatenate([vt, vt], 0)
            )
            qhi, qlo = split(qsum[k])
            g2 = (mm(qhi, cq[...]) + mm(qlo, cq[...])).T
            out_u[k, 0] = g2[:rank] + g2[rank:]
            return carry

        lax.fori_loop(0, slots, one_slot, 0, unroll=2)


def tiles_in_kernel(values, users, items, tsteps, count, blocks, cores):
    slots, unused, rank, width = blocks.shape
    steps = cores.shape[0]
    total = values.shape[0]
    chunk = 64
    group = 16
    ahead = 4
    chi, clo = split_outside(cores)
    flat_hi, flat_lo = chi.reshape(steps * rank, rank), clo.reshape(steps * rank, rank)
    c4 = jnp.concatenate([flat_hi, flat_lo, flat_hi, flat_lo], 1)
    ct2 = jnp.concatenate([flat_hi.T, flat_lo.T], 0)
    turned = jnp.concatenate([jnp.swapaxes(chi, 1, 2), jnp.swapaxes(clo, 1, 2)], 2)
    cq = jnp.concatenate([turned, turned], 1).reshape(steps * 2 * rank, 2 * rank)

    def values_at(i, users, items, tsteps, count):
        last = jnp.maximum((count[0] + chunk - 1) // chunk - 1, 0)
        return (jnp.minimum(i, last), 0, 0)

    whole = pl.BlockSpec(memory_space=pltpu.VMEM)
    return pl.pallas_call(
        functools.partial(tile_kernel, chunk, group, ahead, steps, rank),
        grid_spec=pltpu.PrefetchScalarGridSpec(
            num_scalar_prefetch=4,
            grid=(total // chunk,),
            in_specs=[pl.BlockSpec((chunk, width, width), values_at)] + [whole] * 4,
            out_specs=[whole] * 3,
            scratch_shapes=[
                pltpu.VMEM((slots, 2 * rank, width), jnp.bfloat16),
                pltpu.VMEM((slots, width, 2 * rank), jnp.bfloat16),
                pltpu.VMEM((slots, width, 2 * rank), jnp.bfloat16),
                pltpu.VMEM((slots * steps, 2 * rank, width), jnp.bfloat16),
                pltpu.VMEM((slots, steps * rank, width), jnp.float32),
                pltpu.VMEM((slots, width, steps * 2 * rank), jnp.float32),
            ],
        ),
        out_shape=[
            jax.ShapeDtypeStruct((slots, 1, rank, width), jnp.float32),
            jax.ShapeDtypeStruct((slots, 1, rank, width), jnp.float32),
            jax.ShapeDtypeStruct((steps * rank, 2 * rank), jnp.float32),
        ],
        compiler_params=pltpu.CompilerParams(
            dimension_semantics=("arbitrary",), vmem_limit_bytes=56 * 2**20
        ),
        name="tiles",
    )(users, items, tsteps, count, values, blocks, c4, ct2, cq)


def pick_kernel(held, left, right, out):
    cap = held.shape[1] // 2

    @pl.loop(0, held.shape[0])
    def one_owner(k):
        for c in range(cap):
            out[k, c] = left[held[k, c]]
            out[k, cap + c] = right[held[k, cap + c]]


def owner_kernel(held, terms_u, terms_v, out_left, out_right):
    cap = held.shape[1] // 2
    out_left[...] = jnp.zeros(out_left.shape, jnp.float32)
    out_right[...] = jnp.zeros(out_right.shape, jnp.float32)

    @pl.loop(0, held.shape[0])
    def one_owner(k):
        for c in range(cap):
            out_left[held[k, c]] += user_scale * terms_u[k, c]
            out_right[held[k, cap + c]] += user_scale * terms_v[k, c]


def plain_kernel(body, shapes, held, *arrays, name):
    whole = pl.BlockSpec(memory_space=pltpu.VMEM)
    return pl.pallas_call(
        body,
        in_specs=[pl.BlockSpec(memory_space=pltpu.SMEM)] + [whole] * len(arrays),
        out_specs=[whole] * len(shapes),
        out_shape=[jax.ShapeDtypeStruct(shape, jnp.float32) for shape in shapes],
        compiler_params=pltpu.CompilerParams(vmem_limit_bytes=32 * 2**20),
        name=name,
    )(held, *arrays)


def tiles_in_loop(values_all, users, items, tsteps, count, left_all, right_all, step_cores):
    slots, rank, width = left_all.shape
    step_count = step_cores.shape[0]
    block_size = min(64, values_all.shape[0])
    live_count = count[0]
    step_ids = jnp.arange(step_count, dtype=jnp.int32)

    def one_block(index, carry):
        grad_left, grad_right, step_sums = carry
        start = index * block_size
        values = lax.dynamic_slice_in_dim(values_all, start, block_size, 0).astype(jnp.float32)
        slots_user = lax.dynamic_slice_in_dim(users, start, block_size, 0)
        slots_item = lax.dynamic_slice_in_dim(items, start, block_size, 0)
        local_steps = lax.dynamic_slice_in_dim(tsteps, start, block_size, 0)
        picker = (local_steps[:, None] == step_ids[None, :]).astype(jnp.float32)
        cores = jnp.take(step_cores, local_steps, axis=0)
        left = jnp.take(left_all, slots_user, axis=0)
        right = jnp.take(right_all, slots_item, axis=0)
        live = (start + jnp.arange(block_size, dtype=jnp.int32) < live_count).astype(jnp.float32)
        mixed = jnp.einsum("tpq,tqj->tpj", cores, right, precision=HIGH)
        guess = jnp.einsum("tpi,tpj->tij", left, mixed, precision=HIGH)
        resid = (guess - values) * live[:, None, None]
        grad_u = jnp.einsum("tij,tpj->tpi", resid, mixed, precision=HIGH)
        across = jnp.einsum("tpi,tpq->tqi", left, cores, precision=HIGH)
        grad_v = jnp.einsum("tij,tqi->tqj", resid, across, precision=HIGH)
        inner = jnp.einsum("tpi,tij->tpj", left, resid, precision=HIGH)
        dcore = jnp.einsum("tpj,tqj->tpq", inner, right, precision=HIGH)
        grad_left = grad_left.at[slots_user].add(grad_u)
        grad_right = grad_right.at[slots_item].add(grad_v)
        step_sums = step_sums + jnp.einsum("ts,tpq->spq", picker, dcore, precision=HIGH)
        return (grad_left, grad_right, step_sums)

    carry = (
        jnp.zeros((slots, rank, width), jnp.float32),
        jnp.zeros((slots, rank, width), jnp.float32),
        jnp.zeros((step_count, rank, rank), jnp.float32),
    )
    return lax.fori_loop(0, (live_count + block_size - 1) // block_size, one_block, carry)


def spread(x, axis, count):
    return lax.all_to_all(
        jnp.broadcast_to(x[None], (count,) + x.shape), axis, split_axis=0, concat_axis=0, tiled=True
    )


def shards(
    tile_values,
    tile_users,
    tile_items,
    tile_steps,
    tile_count,
    users_ask,
    items_ask,
    user_factor,
    item_factor,
    time_factor,
    core,
):
    count_tm = lax.axis_size("tm")
    count_rows = lax.axis_size("rows")
    owners = count_tm * count_rows
    cap = users_ask.shape[1]
    rank = user_factor.shape[1]
    width = user_factor.shape[2]
    steps = time_factor.shape[0]
    slots = owners * cap

    exchange = functools.partial(
        lax.all_to_all, axis_name=BOTH, split_axis=0, concat_axis=0, tiled=True
    )
    held = exchange(jnp.concatenate([users_ask, items_ask], 1))
    (found,) = plain_kernel(
        pick_kernel,
        [(owners, 2 * cap, rank, width)],
        held,
        user_factor,
        item_factor,
        name="pick",
    )
    back = exchange(found)
    cores = jnp.einsum("pqr,sr->spq", core, time_factor, precision=HIGH)

    if slots <= 32 and cap == 1 and tile_values.shape[0] % 64 == 0:
        terms_u, terms_v, twice = tiles_in_kernel(
            tile_values, tile_users, tile_items, tile_steps, tile_count, back, cores
        )
        step_sums = twice[:, :rank] + twice[:, rank:]
    else:
        left = back[:, :cap].reshape(slots, rank, width)
        right = back[:, cap:].reshape(slots, rank, width)
        part_u, part_v, step_sums = tiles_in_loop(
            tile_values, tile_users, tile_items, tile_steps, tile_count, left, right, cores
        )
        terms_u = part_u.reshape(owners, cap, rank, width)
        terms_v = part_v.reshape(owners, cap, rank, width)

    back_u = exchange(terms_u)
    share = steps // count_rows
    lanes = share * rank * rank // 128
    own_steps = lax.all_to_all(
        step_sums.reshape(count_rows, lanes, 128), "rows", split_axis=0, concat_axis=0, tiled=True
    ).sum(0)
    own_time = lax.dynamic_slice_in_dim(time_factor, lax.axis_index("rows") * share, share, 0)
    own_time = jnp.pad(own_time.reshape(-1), (0, 8 * 128 - share * rank)).reshape(8, 128)
    piece = jnp.concatenate([own_steps, own_time], 0)
    over_tm = spread(piece, "tm", count_tm)
    terms_v, over_tm = lax.optimization_barrier((terms_v, over_tm))
    back_v = exchange(terms_v)
    every = spread(over_tm, "rows", count_rows)
    time_all = every[:, :, lanes:].reshape(owners, 8 * 128)[:, : share * rank]
    time_all = time_all.reshape(owners * share, rank)
    mine = lax.dynamic_index_in_dim(every, lax.axis_index("tm"), 1, keepdims=False)
    mine = mine[:, :lanes].reshape(steps, rank, rank)
    every = every[:, :, :lanes].reshape(owners * share, rank, rank)
    grad_users, grad_items = plain_kernel(
        owner_kernel, [user_factor.shape, item_factor.shape], held, back_u, back_v, name="owner_sums"
    )
    grad_time = time_scale * jnp.einsum("spq,pqr->sr", mine, core, precision=HIGH)
    grad_core = core_scale * jnp.einsum("spq,sr->pqr", every, time_all, precision=HIGH)
    return (grad_users, grad_items, grad_time, grad_core)


def solution(mesh):
    in_specs = (
        P(BOTH, None, None),
        P(BOTH),
        P(BOTH),
        P(BOTH),
        P(BOTH),
        P(BOTH, None),
        P(BOTH, None),
        P(BOTH, None, None),
        P(BOTH, None, None),
        P("tm", None),
        P(),
    )
    out_specs = (P(BOTH, None, None), P(BOTH, None, None), P("tm", None), P())
    return jax.shard_map(shards, mesh=mesh, in_specs=in_specs, out_specs=out_specs, check_vma=False)
```

```python
import functools

import jax
import jax.numpy as jnp
from jax import lax
from jax.experimental import pallas as pl
from jax.experimental.pallas import tpu as pltpu
from jax.sharding import PartitionSpec as P

HIGH = lax.Precision.HIGHEST
user_scale = 0.125
time_scale = 1.0 / 2048.0
core_scale = 1.0 / 4096.0
BOTH = ("tm", "rows")


def split(x):
    hi = x.astype(jnp.bfloat16)
    lo = (x - hi.astype(jnp.float32)).astype(jnp.bfloat16)
    return hi, lo


def split_outside(x):
    hi = lax.reduce_precision(x, 8, 7)
    return hi.astype(jnp.bfloat16), (x - hi).astype(jnp.bfloat16)


def mm(a, b):
    return jnp.dot(a, b, preferred_element_type=jnp.float32)


def tile_kernel(
    chunk, group, ahead, steps, rank,
    users, items, tsteps, count,
    values, blocks, c4, ct2, cq,
    out, out_d,
    u2, ut2, vt2, m2, psum, qsum,
):
    slots = blocks.shape[0]
    width = blocks.shape[3]
    step = pl.program_id(0)

    @pl.when(step == 0)
    def prepare():
        def one_slot(k, carry):
            hi, lo = split(blocks[k, 0])
            u2[k] = jnp.concatenate([hi, lo], 0)
            both = jnp.concatenate([hi.astype(jnp.float32), lo.astype(jnp.float32)], 0)
            ut2[k] = both.T.astype(jnp.bfloat16)
            hi, lo = split(blocks[k, 1])
            both = jnp.concatenate([hi.astype(jnp.float32), lo.astype(jnp.float32)], 0)
            vt2[k] = both.T.astype(jnp.bfloat16)
            mixed = mm(c4[...], jnp.concatenate([hi, hi, lo, lo], 0))
            mhi, mlo = split(mixed)
            for s in range(steps):
                m2[k * steps + s, 0:rank, :] = mhi[s * rank:(s + 1) * rank]
                m2[k * steps + s, rank:2 * rank, :] = mlo[s * rank:(s + 1) * rank]
            psum[k] = jnp.zeros((steps * rank, width), jnp.float32)
            qsum[k] = jnp.zeros((width, steps * 2 * rank), jnp.float32)
            return carry

        lax.fori_loop(0, slots, one_slot, 0, unroll=2)

    base = step * chunk
    live = jnp.clip(count[0] - base, 0, chunk)

    @pl.loop(0, (live + group - 1) // group)
    def one_group(g):
        first = g * group
        ids = []
        for k in range(group):
            t = base + first + k
            ids.append((users[t], items[t], tsteps[t]))

        def guess_of(k):
            u, v, s = ids[k]
            m = m2[v * steps + s]
            mhi, mlo = m[:rank], m[rank:]
            ut = ut2[u]
            return mm(
                jnp.concatenate([ut, ut], 1), jnp.concatenate([mhi, mhi, mlo, mlo], 0)
            )

        def products_of(k, guess):
            u, v, s = ids[k]
            resid = guess - values[first + k].astype(jnp.float32)
            resid = jnp.where(first + k < live, resid, 0.0)
            rhi, rlo = split(resid)
            ul = u2[u]
            vt = vt2[v]
            w = mm(jnp.concatenate([ul, ul], 1), jnp.concatenate([rhi, rlo], 0))
            z = mm(jnp.concatenate([rhi, rlo], 1), jnp.concatenate([vt, vt], 0))
            return w[:rank] + w[rank:], z

        def add_up(k, w, z):
            u, v, s = ids[k]
            at_p = pl.ds(pl.multiple_of(s * rank, rank), rank)
            psum[v, at_p, :] += w
            at_q = pl.ds(pl.multiple_of(s * 2 * rank, 2 * rank), 2 * rank)
            qsum[u, :, at_q] += z

        guesses, products = {}, {}
        for k in range(group + ahead + 2):
            if k < group:
                guesses[k] = guess_of(k)
            if 0 <= k - ahead < group:
                products[k - ahead] = products_of(k - ahead, guesses.pop(k - ahead))
            if 0 <= k - ahead - 2 < group:
                add_up(k - ahead - 2, *products.pop(k - ahead - 2))

    @pl.when(step == pl.num_programs(0) - 1)
    def finish():
        out_d[...] = jnp.zeros(out_d.shape, jnp.float32)

        def one_slot(k, carry):
            hi, lo = split(psum[k])
            g1 = mm(ct2[...], hi)
            out[k, 1] = g1[:rank] + g1[rank:] + mm(ct2[0:rank, :], lo)
            vt = vt2[k]
            out_d[...] += mm(
                jnp.concatenate([hi, lo], 1), jnp.concatenate([vt, vt], 0)
            )
            qhi, qlo = split(qsum[k])
            g2 = (mm(qhi, cq[...]) + mm(qlo, cq[...])).T
            out[k, 0] = g2[:rank] + g2[rank:]
            return carry

        lax.fori_loop(0, slots, one_slot, 0, unroll=2)


def tiles_in_kernel(values, users, items, tsteps, count, blocks, cores):
    slots, unused, rank, width = blocks.shape
    steps = cores.shape[0]
    total = values.shape[0]
    chunk = 64
    group = 16
    ahead = 4
    chi, clo = split_outside(cores)
    flat_hi, flat_lo = chi.reshape(steps * rank, rank), clo.reshape(steps * rank, rank)
    c4 = jnp.concatenate([flat_hi, flat_lo, flat_hi, flat_lo], 1)
    ct2 = jnp.concatenate([flat_hi.T, flat_lo.T], 0)
    turned = jnp.concatenate([jnp.swapaxes(chi, 1, 2), jnp.swapaxes(clo, 1, 2)], 2)
    cq = jnp.concatenate([turned, turned], 1).reshape(steps * 2 * rank, 2 * rank)

    def values_at(i, users, items, tsteps, count):
        last = jnp.maximum((count[0] + chunk - 1) // chunk - 1, 0)
        return (jnp.minimum(i, last), 0, 0)

    whole = pl.BlockSpec(memory_space=pltpu.VMEM)
    return pl.pallas_call(
        functools.partial(tile_kernel, chunk, group, ahead, steps, rank),
        grid_spec=pltpu.PrefetchScalarGridSpec(
            num_scalar_prefetch=4,
            grid=(total // chunk,),
            in_specs=[pl.BlockSpec((chunk, width, width), values_at)] + [whole] * 4,
            out_specs=[whole] * 2,
            scratch_shapes=[
                pltpu.VMEM((slots, 2 * rank, width), jnp.bfloat16),
                pltpu.VMEM((slots, width, 2 * rank), jnp.bfloat16),
                pltpu.VMEM((slots, width, 2 * rank), jnp.bfloat16),
                pltpu.VMEM((slots * steps, 2 * rank, width), jnp.bfloat16),
                pltpu.VMEM((slots, steps * rank, width), jnp.float32),
                pltpu.VMEM((slots, width, steps * 2 * rank), jnp.float32),
            ],
        ),
        out_shape=[
            jax.ShapeDtypeStruct(blocks.shape, jnp.float32),
            jax.ShapeDtypeStruct((steps * rank, 2 * rank), jnp.float32),
        ],
        compiler_params=pltpu.CompilerParams(
            dimension_semantics=("arbitrary",), vmem_limit_bytes=56 * 2**20
        ),
        name="tiles",
    )(users, items, tsteps, count, values, blocks, c4, ct2, cq)


def pick_kernel(held, left, right, out):
    cap = held.shape[1] // 2

    @pl.loop(0, held.shape[0])
    def one_owner(k):
        for c in range(cap):
            out[k, c] = left[held[k, c]]
            out[k, cap + c] = right[held[k, cap + c]]


def owner_kernel(held, terms, out_left, out_right):
    cap = held.shape[1] // 2
    out_left[...] = jnp.zeros(out_left.shape, jnp.float32)
    out_right[...] = jnp.zeros(out_right.shape, jnp.float32)

    @pl.loop(0, held.shape[0])
    def one_owner(k):
        for c in range(cap):
            out_left[held[k, c]] += user_scale * terms[k, c]
            out_right[held[k, cap + c]] += user_scale * terms[k, cap + c]


def plain_kernel(body, shapes, held, *arrays, name):
    whole = pl.BlockSpec(memory_space=pltpu.VMEM)
    return pl.pallas_call(
        body,
        in_specs=[pl.BlockSpec(memory_space=pltpu.SMEM)] + [whole] * len(arrays),
        out_specs=[whole] * len(shapes),
        out_shape=[jax.ShapeDtypeStruct(shape, jnp.float32) for shape in shapes],
        compiler_params=pltpu.CompilerParams(vmem_limit_bytes=32 * 2**20),
        name=name,
    )(held, *arrays)


def tiles_in_loop(values_all, users, items, tsteps, count, left_all, right_all, step_cores):
    slots, rank, width = left_all.shape
    step_count = step_cores.shape[0]
    block_size = min(64, values_all.shape[0])
    live_count = count[0]
    step_ids = jnp.arange(step_count, dtype=jnp.int32)

    def one_block(index, carry):
        grad_left, grad_right, step_sums = carry
        start = index * block_size
        values = lax.dynamic_slice_in_dim(values_all, start, block_size, 0).astype(jnp.float32)
        slots_user = lax.dynamic_slice_in_dim(users, start, block_size, 0)
        slots_item = lax.dynamic_slice_in_dim(items, start, block_size, 0)
        local_steps = lax.dynamic_slice_in_dim(tsteps, start, block_size, 0)
        picker = (local_steps[:, None] == step_ids[None, :]).astype(jnp.float32)
        cores = jnp.take(step_cores, local_steps, axis=0)
        left = jnp.take(left_all, slots_user, axis=0)
        right = jnp.take(right_all, slots_item, axis=0)
        live = (start + jnp.arange(block_size, dtype=jnp.int32) < live_count).astype(jnp.float32)
        mixed = jnp.einsum("tpq,tqj->tpj", cores, right, precision=HIGH)
        guess = jnp.einsum("tpi,tpj->tij", left, mixed, precision=HIGH)
        resid = (guess - values) * live[:, None, None]
        grad_u = jnp.einsum("tij,tpj->tpi", resid, mixed, precision=HIGH)
        across = jnp.einsum("tpi,tpq->tqi", left, cores, precision=HIGH)
        grad_v = jnp.einsum("tij,tqi->tqj", resid, across, precision=HIGH)
        inner = jnp.einsum("tpi,tij->tpj", left, resid, precision=HIGH)
        dcore = jnp.einsum("tpj,tqj->tpq", inner, right, precision=HIGH)
        grad_left = grad_left.at[slots_user].add(grad_u)
        grad_right = grad_right.at[slots_item].add(grad_v)
        step_sums = step_sums + jnp.einsum("ts,tpq->spq", picker, dcore, precision=HIGH)
        return (grad_left, grad_right, step_sums)

    carry = (
        jnp.zeros((slots, rank, width), jnp.float32),
        jnp.zeros((slots, rank, width), jnp.float32),
        jnp.zeros((step_count, rank, rank), jnp.float32),
    )
    return lax.fori_loop(0, (live_count + block_size - 1) // block_size, one_block, carry)


def spread(x, axis, count):
    return lax.all_to_all(
        jnp.broadcast_to(x[None], (count,) + x.shape), axis, split_axis=0, concat_axis=0, tiled=True
    )


def shards(
    tile_values,
    tile_users,
    tile_items,
    tile_steps,
    tile_count,
    users_ask,
    items_ask,
    user_factor,
    item_factor,
    time_factor,
    core,
):
    count_tm = lax.axis_size("tm")
    count_rows = lax.axis_size("rows")
    owners = count_tm * count_rows
    cap = users_ask.shape[1]
    rank = user_factor.shape[1]
    width = user_factor.shape[2]
    steps = time_factor.shape[0]
    slots = owners * cap

    exchange = functools.partial(
        lax.all_to_all, axis_name=BOTH, split_axis=0, concat_axis=0, tiled=True
    )
    held = exchange(jnp.concatenate([users_ask, items_ask], 1))
    (found,) = plain_kernel(
        pick_kernel,
        [(owners, 2 * cap, rank, width)],
        held,
        user_factor,
        item_factor,
        name="pick",
    )
    back = exchange(found)
    cores = jnp.einsum("pqr,sr->spq", core, time_factor, precision=HIGH)

    if slots <= 32 and cap == 1 and tile_values.shape[0] % 64 == 0:
        terms, twice = tiles_in_kernel(
            tile_values, tile_users, tile_items, tile_steps, tile_count, back, cores
        )
        step_sums = twice[:, :rank] + twice[:, rank:]
    else:
        left = back[:, :cap].reshape(slots, rank, width)
        right = back[:, cap:].reshape(slots, rank, width)
        part_u, part_v, step_sums = tiles_in_loop(
            tile_values, tile_users, tile_items, tile_steps, tile_count, left, right, cores
        )
        terms = jnp.concatenate(
            [part_u.reshape(owners, cap, rank, width), part_v.reshape(owners, cap, rank, width)], 1
        )

    share = steps // count_rows
    lanes = share * rank * rank // 128
    own_steps = lax.all_to_all(
        step_sums.reshape(count_rows, lanes, 128), "rows", split_axis=0, concat_axis=0, tiled=True
    ).sum(0)
    own_time = lax.dynamic_slice_in_dim(time_factor, lax.axis_index("rows") * share, share, 0)
    own_time = jnp.pad(own_time.reshape(-1), (0, 8 * 128 - share * rank)).reshape(8, 128)
    piece = jnp.concatenate([own_steps, own_time], 0)
    over_tm = spread(piece, "tm", count_tm)
    returned = exchange(terms)
    every = spread(over_tm, "rows", count_rows)
    time_all = every[:, :, lanes:].reshape(owners, 8 * 128)[:, : share * rank]
    time_all = time_all.reshape(owners * share, rank)
    mine = lax.dynamic_index_in_dim(every, lax.axis_index("tm"), 1, keepdims=False)
    mine = mine[:, :lanes].reshape(steps, rank, rank)
    every = every[:, :, :lanes].reshape(owners * share, rank, rank)
    grad_users, grad_items = plain_kernel(
        owner_kernel, [user_factor.shape, item_factor.shape], held, returned, name="owner_sums"
    )
    grad_time = time_scale * jnp.einsum("spq,pqr->sr", mine, core, precision=HIGH)
    grad_core = core_scale * jnp.einsum("spq,sr->pqr", every, time_all, precision=HIGH)
    return (grad_users, grad_items, grad_time, grad_core)


def solution(mesh):
    in_specs = (
        P(BOTH, None, None),
        P(BOTH),
        P(BOTH),
        P(BOTH),
        P(BOTH),
        P(BOTH, None),
        P(BOTH, None),
        P(BOTH, None, None),
        P(BOTH, None, None),
        P("tm", None),
        P(),
    )
    out_specs = (P(BOTH, None, None), P(BOTH, None, None), P("tm", None), P())
    return jax.shard_map(shards, mesh=mesh, in_specs=in_specs, out_specs=out_specs, check_vma=False)
```
